32 devices in a mesh: kv: 4 (over z), blk: 8 (over y, x, core).
Axes of the slice: x: 2, y: 2, z: 4, core: 2. Of those that a mesh axis runs over, the one named last changes fastest.
Arguments:
- embeds: bfloat16 [1, 64, 3072], P(None, None, 'blk'), may hold values from -40 to 40
- attn_norm: float32 [3072], P('blk'), may hold values from 0.25 to 1.75
- query_key_value_weight: bfloat16 [3072, 5120], P('blk', 'kv'), may hold values from -0.109375 to 0.109375
- w_out: bfloat16 [3072, 3072], P('kv', 'blk'), may hold values from -0.109375 to 0.109375
- mlp_norm: float32 [3072], P('blk'), may hold values from 0.25 to 1.75
- w_gate: bfloat16 [3072, 8192], P('blk', 'kv'), may hold values from -0.109375 to 0.109375
- w_up: bfloat16 [3072, 8192], P('blk', 'kv'), may hold values from -0.109375 to 0.109375
- w_down: bfloat16 [8192, 3072], P('kv', 'blk'), may hold values from -0.0625 to 0.0625
- prompt_key_slots: bfloat16 [256, 8, 128, 128], P('blk', 'kv'), may hold values from -210 to 210
- prompt_value_slots: bfloat16 [256, 8, 128, 128], P('blk', 'kv'), may hold values from -6 to 6
- generated_keys: bfloat16 [64, 8, 127, 128], P('blk', 'kv'), may hold values from -10 to 10
- generated_values: bfloat16 [64, 8, 127, 128], P('blk', 'kv'), may hold values from -6 to 6
- parents: int32 [1, 64], P(None, 'blk'), may hold values from 0 to 7
- prompt_length: int32 [8], replicated, may hold values from 1024 to 8192
- tenant_bounds: int32 [5], replicated, may hold values from 0 to 8, as said below
- slot_table: int32 [256], P('blk'), may hold values from 0 to 256, as said below
Outputs:
- hidden_out: float32 [1, 64, 3072], P(None, None, 'blk')
- keys_out: bfloat16 [64, 8, 128, 128], P('blk', 'kv')
- values_out: bfloat16 [64, 8, 128, 128], P('blk', 'kv')
The draws below stay inside these ranges and needn't reach their ends.
Inputs may be any that keep to these rules, and one draw needn't show every extreme that they name: parents[s, b] is the beam, among the 8 beams of b's request, whose cache beam b continues at step s. tenant_bounds[0] = 0 and tenant_bounds[4] = 8, strictly rising. `slot_table`: with L_t the largest prompt_length of tenant t's requests, every block j below ceil(L_t / 128) of every tenant t stands in exactly one slot as t * 64 + j, no other block stands anywhere, and 256 marks an empty slot.
All inputs are finite; a program needn't handle non-finite values.
Results may differ from the reference program's by a relative error of at most 0.012.
The reference program's roundings to bfloat16 on the way count: a program that leaves them out, or rounds other values in their place, can miss the bound.
Values may be sent and summed in bfloat16 or wider, within the bound.
A program may use at most 64 MiB of HBM per device.

```python
import math
import jax
import jax.numpy as jnp
from jax import lax

MODEL_WIDTH = 3072
QUERY_HEADS = 24
KEY_VALUE_HEADS = 8
HEAD_WIDTH = 128
FF = 8192
GROUP_HEADS = 3
REQUEST_BEAMS = 8
TENANT_COUNT = 4
REQUEST_COUNT = 8
TOTAL_BEAMS = 64
PROMPT_POSITIONS = 8192
BLOCK_POSITIONS = 128
PROMPT_BLOCKS = 64
BLOCK_SLOTS = 256
EARLIER_TOKENS = 127
DECODE_STEPS = 1
GENERATED_LENGTH = 128


def layout_tables(key):
    random_subkeys = jax.random.split(jax.random.fold_in(key, 29), 4)
    cuts = jnp.sort(jax.random.permutation(random_subkeys[0], REQUEST_COUNT - 1)[:TENANT_COUNT - 1] + 1).astype(jnp.int32)
    bounds = jnp.concatenate([jnp.zeros((1,), jnp.int32), cuts, jnp.full((1,), REQUEST_COUNT, jnp.int32)])
    request_ids = jnp.arange(REQUEST_COUNT, dtype=jnp.int32)
    lengths = jax.random.randint(random_subkeys[1], (REQUEST_COUNT,), PROMPT_POSITIONS // 8, PROMPT_POSITIONS - BLOCK_POSITIONS + 1)
    picks = jax.random.permutation(random_subkeys[2], REQUEST_COUNT)
    lengths = jnp.where(request_ids == picks[0], PROMPT_POSITIONS, lengths)
    lengths = jnp.where(request_ids == picks[1], PROMPT_POSITIONS // 8, lengths).astype(jnp.int32)
    request_tenant = jnp.sum((request_ids[:, None] >= bounds[None, 1:TENANT_COUNT]).astype(jnp.int32), axis=1)
    longest = jnp.max(jnp.where(request_tenant[:, None] == jnp.arange(TENANT_COUNT, dtype=jnp.int32)[None, :], lengths[:, None], 0), axis=0)
    needed = (longest + BLOCK_POSITIONS - 1) // BLOCK_POSITIONS
    block_ids = jnp.arange(BLOCK_SLOTS, dtype=jnp.int32)
    valid = block_ids % PROMPT_BLOCKS < needed[block_ids // PROMPT_BLOCKS]
    order = jnp.argsort(1 - valid.astype(jnp.int32), stable=True)
    filled = jnp.sum(valid.astype(jnp.int32))
    entries = jnp.where(block_ids < filled, block_ids[order], BLOCK_SLOTS).astype(jnp.int32)
    places = jax.random.permutation(random_subkeys[3], BLOCK_SLOTS)
    table = jnp.zeros((BLOCK_SLOTS,), jnp.int32).at[places].set(entries)
    return (bounds, lengths, table)


def draw_tenant_bounds(key, part):
    return layout_tables(key)[0]


def draw_prompt_length(key, part):
    return layout_tables(key)[1]


def draw_slot_table(key, part):
    return layout_tables(key)[2]


def draw_embeds(key, part):
    random_subkeys = jax.random.split(jax.random.fold_in(key, 11), 4)
    row_scale = jnp.exp(jax.random.uniform(random_subkeys[0], (DECODE_STEPS, TOTAL_BEAMS, 1), jnp.float32, -0.8, 0.8))
    rough_scale = jnp.exp(jax.random.uniform(random_subkeys[1], (1, 1, MODEL_WIDTH), jnp.float32, -0.35, 0.35))
    column_frac = jnp.arange(MODEL_WIDTH, dtype=jnp.float32)[None, None, :] / (MODEL_WIDTH - 1.0) - 0.5
    ramp_scale = jnp.exp(column_frac * math.log(4.0))
    base_draw = jnp.clip(jax.random.normal(random_subkeys[3], (DECODE_STEPS, TOTAL_BEAMS, MODEL_WIDTH), jnp.float32), -4.0, 4.0)
    return (base_draw * row_scale * rough_scale * ramp_scale).astype(jnp.bfloat16)


def draw_prompt_key_slots(key, part):
    random_subkeys = jax.random.split(jax.random.fold_in(key, 13), 1)
    complete_shape = (BLOCK_SLOTS, KEY_VALUE_HEADS, BLOCK_POSITIONS, HEAD_WIDTH)
    result = jnp.clip(2.0 * jax.random.normal(random_subkeys[0], complete_shape, jnp.float32), -10.0, 10.0)
    return result.astype(jnp.bfloat16)


def with_ends(array, own_key, smallest, top_value):
    shape = array.shape
    place = [jax.random.randint(jax.random.fold_in(own_key, axis), (), 0, shape[axis]) for axis in range(len(shape))]
    array = array.at[tuple(place)].set(smallest)
    longest = shape.index(max(shape))
    place[longest] = (place[longest] + 1) % shape[longest]
    return array.at[tuple(place)].set(top_value)


def block_levels(own_key, extent, shards, least, top_value):
    level, own = 1.0, jax.random.fold_in(own_key, 6)
    for dim, shards_of in shards:
        draws = jnp.exp(jax.random.uniform(jax.random.fold_in(own, dim), (shards_of,), jnp.float32, least / len(shards), top_value / len(shards)))
        level = level * jnp.repeat(draws, extent[dim] // shards_of).reshape([-1 if axis == dim else 1 for axis in range(len(extent))])
    return level


def normal_values(key, dims, deviation, most, cuts=(), held_as=jnp.bfloat16):
    values = deviation * jax.random.normal(key, dims, jnp.float32)
    if cuts:
        values = values * block_levels(key, dims, cuts, -0.22, 0.18)
    return jnp.clip(values, -most, most).astype(held_as)


def setup_inputs(seed: int = 0) -> dict:
    keys = jax.random.split(jax.random.key(seed), 17)
    return {
        "embeds": draw_embeds(jax.random.fold_in(keys[16], 71), 0),
        "attn_norm": jnp.clip(1.0 + 0.15 * jax.random.normal(keys[1], (MODEL_WIDTH,), jnp.float32), 0.25, 1.75),
        "query_key_value_weight": normal_values(keys[2], (MODEL_WIDTH, KEY_VALUE_HEADS * (GROUP_HEADS + 2) * HEAD_WIDTH), MODEL_WIDTH ** -0.5, 0.109375, ((0, 8), (1, 4))),
        "w_out": normal_values(keys[3], (QUERY_HEADS * HEAD_WIDTH, MODEL_WIDTH), (QUERY_HEADS * HEAD_WIDTH) ** -0.5, 0.109375, ((0, 4), (1, 8))),
        "mlp_norm": jnp.clip(1.0 + 0.15 * jax.random.normal(keys[4], (MODEL_WIDTH,), jnp.float32), 0.25, 1.75),
        "w_gate": normal_values(keys[5], (MODEL_WIDTH, FF), MODEL_WIDTH ** -0.5, 0.109375, ((0, 8), (1, 4))),
        "w_up": normal_values(keys[6], (MODEL_WIDTH, FF), MODEL_WIDTH ** -0.5, 0.109375, ((0, 8), (1, 4))),
        "w_down": normal_values(keys[7], (FF, MODEL_WIDTH), FF ** -0.5, 0.0625, ((0, 4), (1, 8))),
        "prompt_key_slots": draw_prompt_key_slots(jax.random.fold_in(keys[16], 71), 0),
        "prompt_value_slots": normal_values(keys[9], (BLOCK_SLOTS, KEY_VALUE_HEADS, BLOCK_POSITIONS, HEAD_WIDTH), 1.0, 6.0, ((0, 8), (1, 4))),
        "generated_keys": normal_values(keys[10], (TOTAL_BEAMS, KEY_VALUE_HEADS, EARLIER_TOKENS, HEAD_WIDTH), 2.0, 10.0, ((0, 8), (1, 4))),
        "generated_values": normal_values(keys[11], (TOTAL_BEAMS, KEY_VALUE_HEADS, EARLIER_TOKENS, HEAD_WIDTH), 1.0, 6.0, ((0, 8), (1, 4))),
        "parents": with_ends(jax.random.randint(keys[12], (DECODE_STEPS, TOTAL_BEAMS), 0, REQUEST_BEAMS), jax.random.fold_in(keys[12], 1), 0, REQUEST_BEAMS - 1).astype(jnp.int32),
        "prompt_length": draw_prompt_length(jax.random.fold_in(keys[16], 71), 0),
        "tenant_bounds": draw_tenant_bounds(jax.random.fold_in(keys[16], 71), 0),
        "slot_table": draw_slot_table(jax.random.fold_in(keys[16], 71), 0),
    }


masked_score = -1e+30

def rotate(values, angles):
    half = values.shape[-1] // 2
    first = values[..., :half]
    second = values[..., half:]
    cosine = jnp.cos(angles)
    sine = jnp.sin(angles)
    return jnp.concatenate([first * cosine - second * sine, second * cosine + first * sine], axis=-1)

def angles_for(positions, head_size):
    half = head_size // 2
    freq = jnp.exp(jnp.arange(half, dtype=jnp.float32) * (-math.log(500000.0) / half))
    return positions.astype(jnp.float32)[:, None] * freq[None, :]

def reference(embeds, attn_norm, query_key_value_weight, w_out, mlp_norm, w_gate, w_up, w_down, prompt_key_slots, prompt_value_slots, generated_keys, generated_values, parents, prompt_length, tenant_bounds, slot_table):
    group_queries = QUERY_HEADS // KEY_VALUE_HEADS
    score_scale = 1.0 / math.sqrt(HEAD_WIDTH)
    request_ids = jnp.arange(REQUEST_COUNT, dtype=jnp.int32)
    request_tenant = lax.optimization_barrier(jnp.sum((request_ids[:, None] >= tenant_bounds[None, 1:TENANT_COUNT]).astype(jnp.int32), axis=1))
    placeholder_array = jnp.zeros((BLOCK_SLOTS + 1,), jnp.int32).at[slot_table].set(jnp.arange(BLOCK_SLOTS, dtype=jnp.int32))[:BLOCK_SLOTS]
    ordered_key_rows = prompt_key_slots[placeholder_array].reshape(TENANT_COUNT, PROMPT_BLOCKS, KEY_VALUE_HEADS, BLOCK_POSITIONS, HEAD_WIDTH).transpose(0, 2, 1, 3, 4).reshape(TENANT_COUNT, KEY_VALUE_HEADS, PROMPT_POSITIONS, HEAD_WIDTH)
    ordered_value_rows = prompt_value_slots[placeholder_array].reshape(TENANT_COUNT, PROMPT_BLOCKS, KEY_VALUE_HEADS, BLOCK_POSITIONS, HEAD_WIDTH).transpose(0, 2, 1, 3, 4).reshape(TENANT_COUNT, KEY_VALUE_HEADS, PROMPT_POSITIONS, HEAD_WIDTH)
    beam_req = jnp.arange(TOTAL_BEAMS, dtype=jnp.int32) // REQUEST_BEAMS
    length_beam = prompt_length[beam_req]
    trailing_zeros = jnp.zeros((TOTAL_BEAMS, KEY_VALUE_HEADS, DECODE_STEPS, HEAD_WIDTH), jnp.bfloat16)
    cached_key_rows = jnp.concatenate([generated_keys, trailing_zeros], axis=2)
    cached_value_rows = jnp.concatenate([generated_values, trailing_zeros], axis=2)
    key_pos = jnp.arange(PROMPT_POSITIONS, dtype=jnp.int32)
    gen_pos = jnp.arange(GENERATED_LENGTH, dtype=jnp.int32)
    outputs = []
    for step in range(DECODE_STEPS):
        residual = embeds[step].astype(jnp.float32)
        inverse = lax.rsqrt(lax.optimization_barrier(jnp.mean(residual * residual, axis=1)) + 1e-05)
        normed = (residual * attn_norm).astype(jnp.bfloat16)
        projected_rows = jnp.dot(normed, query_key_value_weight, preferred_element_type=jnp.float32) * inverse[:, None]
        projected_rows = projected_rows.reshape(TOTAL_BEAMS, KEY_VALUE_HEADS, group_queries + 2, HEAD_WIDTH)
        angles = angles_for(length_beam + EARLIER_TOKENS + step, HEAD_WIDTH)
        query_rows = rotate(projected_rows[:, :, :group_queries], angles[:, None, None, :]).astype(jnp.bfloat16)
        new_key = rotate(projected_rows[:, :, group_queries], angles[:, None, :]).astype(jnp.bfloat16)
        new_value = projected_rows[:, :, group_queries + 1].astype(jnp.bfloat16)
        parent_rows = beam_req * REQUEST_BEAMS + parents[step]
        cached_key_rows = cached_key_rows[parent_rows].at[:, :, EARLIER_TOKENS + step].set(new_key)
        cached_value_rows = cached_value_rows[parent_rows].at[:, :, EARLIER_TOKENS + step].set(new_value)

        def attend_heads(items):
            query, keys_gen, values_gen, length, tenant = items
            query_f = query.astype(jnp.float32)
            tenant_keys = ordered_key_rows[tenant].astype(jnp.float32)
            tenant_values = ordered_value_rows[tenant].astype(jnp.float32)
            prompt_scores = jnp.einsum('bkgd,knd->bkgn', query_f, tenant_keys) * score_scale
            gen_scores = jnp.einsum('bkgd,bknd->bkgn', query_f, keys_gen.astype(jnp.float32)) * score_scale
            scores = jnp.concatenate([prompt_scores, gen_scores], axis=3)
            mask = jnp.concatenate([key_pos < length, gen_pos <= EARLIER_TOKENS + step])[None, None, None, :]
            top_score = lax.optimization_barrier(jnp.max(jnp.where(mask, scores, masked_score), axis=3, keepdims=True))
            weights = jnp.where(mask, jnp.exp(scores - top_score), 0.0)
            total_mass = lax.optimization_barrier(jnp.sum(weights, axis=3, keepdims=True))
            rounded = lax.optimization_barrier(weights.astype(jnp.bfloat16)).astype(jnp.float32)
            summed = jnp.einsum('bkgn,knd->bkgd', rounded[..., :PROMPT_POSITIONS], tenant_values)
            summed = summed + jnp.einsum('bkgn,bknd->bkgd', rounded[..., PROMPT_POSITIONS:], values_gen.astype(jnp.float32))
            return (summed / total_mass).astype(jnp.bfloat16)
        attended_output = lax.map(attend_heads, (query_rows.reshape(REQUEST_COUNT, REQUEST_BEAMS, KEY_VALUE_HEADS, group_queries, HEAD_WIDTH), cached_key_rows.reshape(REQUEST_COUNT, REQUEST_BEAMS, KEY_VALUE_HEADS, GENERATED_LENGTH, HEAD_WIDTH), cached_value_rows.reshape(REQUEST_COUNT, REQUEST_BEAMS, KEY_VALUE_HEADS, GENERATED_LENGTH, HEAD_WIDTH), prompt_length, request_tenant))
        heads_out = attended_output.reshape(TOTAL_BEAMS, QUERY_HEADS * HEAD_WIDTH)
        after_attn = residual + jnp.dot(heads_out, w_out, preferred_element_type=jnp.float32)
        inverse2 = lax.rsqrt(lax.optimization_barrier(jnp.mean(after_attn * after_attn, axis=1)) + 1e-05)
        normed2 = (after_attn * mlp_norm).astype(jnp.bfloat16)
        gate = jnp.dot(normed2, w_gate, preferred_element_type=jnp.float32) * inverse2[:, None]
        upper = jnp.dot(normed2, w_up, preferred_element_type=jnp.float32) * inverse2[:, None]
        hidden = (jax.nn.silu(gate) * upper).astype(jnp.bfloat16)
        outputs.append(after_attn + jnp.dot(hidden, w_down, preferred_element_type=jnp.float32))
    return (jnp.stack(outputs), cached_key_rows, cached_value_rows)
```

```python
import functools
import math

import jax
import jax.numpy as jnp
from jax import lax
from jax.experimental import pallas as pl
from jax.experimental.pallas import tpu as pltpu
from jax.sharding import PartitionSpec as P

MODEL_WIDTH = 3072
GROUP = 3
HEAD = 128
BEAMS = 8
TENANTS = 4
BLOCK = 128
PROMPT = 8192
EARLIER = 127
COLS = (GROUP + 2) * HEAD
MASKED = -1e30
FLOOR = -1e29
MESH = pl.DeviceIdType.MESH
F32 = jnp.float32
BF16 = jnp.bfloat16


def split3(column, shape):
    hi = column.astype(BF16).astype(F32)
    rest = column - hi
    mid = rest.astype(BF16).astype(F32)
    low = rest - mid
    lane = lax.broadcasted_iota(jnp.int32, shape, len(shape) - 1)
    return jnp.where(lane == 0, hi, jnp.where(lane == 1, mid, jnp.where(lane == 2, low, 0.0)))


def dot_t(a, b):
    return lax.dot_general(a, b, (((1,), (1,)), ((), ())), preferred_element_type=F32)


def kernel(
    n, z, hk, slots, width, units,
    parents, lengths, bounds, table,
    embeds, attn_norm, mlp_norm,
    wqkv_h, wout_h, wgate_h, wup_h, wdown_h, pk_h, pv_h, gk_h, gv_h,
    hidden_out, keys_out, values_out,
    wqkv, wout, wgate, wup, wdown, pk, pv, gk, gv, local_sem,
    qs, qr, qall, os_, orx, oall, ys, kr, gs, gr, hall, fs, fr,
    low_b, high_b, sbuf, tmp,
    s1, r1, s2, r2, s3, r3, s4, r4, s5, r5, s6, r6, s7, r7, s8, r8,
):
    b = lax.axis_index("blk")
    k = lax.axis_index("kv")
    rows = n * BEAMS
    own_q = hk * GROUP * BEAMS
    per_head = GROUP * BEAMS
    scale = 1.0 / math.sqrt(HEAD)

    loads = [
        pltpu.make_async_copy(src, dst, local_sem.at[i])
        for i, (src, dst) in enumerate(
            [(wqkv_h, wqkv), (gk_h, gk), (gv_h, gv), (pk_h, pk), (pv_h, pv),
             (wout_h, wout), (wgate_h, wgate), (wup_h, wup), (wdown_h, wdown)]
        )
    ]
    for load in loads:
        load.start()
    l_qkv, l_gk, l_gv, l_pk, l_pv, l_out, l_gate, l_up, l_down = loads

    barrier = pltpu.get_barrier_semaphore()

    @pl.loop(1, n)
    def _(d):
        pl.semaphore_signal(barrier, inc=1, device_id={"blk": lax.rem(b + d, n)}, device_id_type=MESH)

    @pl.loop(1, z)
    def _(d):
        pl.semaphore_signal(barrier, inc=1, device_id={"kv": lax.rem(k + d, z)}, device_id_type=MESH)

    def exchange(axis, me, size, src_of, dst, ssem, rsem):
        def copy(other, slot):
            return pltpu.make_async_remote_copy(
                src_ref=src_of(other), dst_ref=dst.at[slot], send_sem=ssem.at[other],
                recv_sem=rsem.at[slot], device_id={axis: other}, device_id_type=MESH,
            )

        def start():
            @pl.loop(1, size)
            def _(d):
                copy(lax.rem(me + d, size), me).start()

        def arrived():
            @pl.loop(1, size)
            def _(d):
                other = lax.rem(me + d, size)
                copy(other, other).wait_recv()

        def sent():
            @pl.loop(1, size)
            def _(d):
                other = lax.rem(me + d, size)
                copy(other, other).wait_send()

        return start, arrived, sent

    blk = functools.partial(exchange, "blk", b, n)
    kvx = functools.partial(exchange, "kv", k, z)
    x_qkv = blk(lambda t: qs.at[t], qr, s1, r1)
    x_q = blk(lambda t: qall.at[b], qall, s2, r2)
    x_o = blk(lambda t: os_.at[t], orx, s3, r3)
    x_heads = blk(lambda t: oall.at[b], oall, s4, r4)
    x_attn = kvx(lambda t: kr.at[k], kr, s5, r5)
    x_mix = blk(lambda t: gs.at[t], gr, s6, r6)
    x_hid = blk(lambda t: hall.at[b], hall, s7, r7)
    x_ff = kvx(lambda t: fr.at[k], fr, s8, r8)

    residual = embeds[0].astype(F32)
    squares = jnp.sum(residual * residual, axis=1, keepdims=True)
    normed = (residual * attn_norm[...]).astype(BF16)
    l_qkv.wait()
    part = jnp.dot(normed, wqkv[...], preferred_element_type=F32)
    qs[:, :, : hk * COLS] = part.reshape(n, BEAMS, hk * COLS)
    qs[:, :, hk * COLS :] = jnp.broadcast_to(squares, (rows, HEAD)).reshape(n, BEAMS, HEAD)
    pl.semaphore_wait(barrier, n - 1 + z - 1)
    x_qkv[0]()

    @pl.loop(0, n)
    def _(t):
        tenant = sum((t >= bounds[i]).astype(jnp.int32) for i in range(1, TENANTS))
        first = tenant * PROMPT
        low_b[t] = jnp.full((per_head, HEAD), first, jnp.int32)
        high_b[t] = jnp.full((per_head, HEAD), first + lengths[t], jnp.int32)

    lane = lax.broadcasted_iota(jnp.int32, (BEAMS, HEAD), 1)
    half = HEAD // 2
    index = jnp.where(lane < half, lane, lane - half).astype(F32)
    freq = jnp.exp(index * (-math.log(500000.0) / half))
    position = jnp.full((BEAMS, HEAD), lengths[b] + EARLIER, jnp.int32).astype(F32)
    angle = position * freq
    cosine = jnp.cos(angle)
    sine = jnp.where(lane < half, -jnp.sin(angle), jnp.sin(angle))

    def rotated(u):
        return u * cosine + pltpu.roll(u, half, 1) * sine

    qr[b] = qs[b]
    x_qkv[1]()
    total = qr[0]
    for t in range(1, n):
        total = total + qr[t]
    inverse = lax.rsqrt(total[:, hk * COLS :] / MODEL_WIDTH + 1e-05)

    def piece(h, j):
        start = h * COLS + j * HEAD
        return total[:, start : start + HEAD] * inverse

    own_query = jnp.concatenate(
        [rotated(piece(h, g)) for h in range(hk) for g in range(GROUP)], axis=0
    ).astype(BF16)
    qall[b] = own_query
    x_q[0]()

    l_gk.wait()
    l_gv.wait()
    row = lax.broadcasted_iota(jnp.int32, (BLOCK, HEAD), 0)
    new = [
        ([rotated(piece(h, GROUP)) for h in range(hk)], gk, keys_out),
        ([piece(h, GROUP + 1) for h in range(hk)], gv, values_out),
    ]
    for i in range(BEAMS):
        parent = parents[0, i]
        for j, (rows_new, src, dst) in enumerate(new):
            for h in range(hk):
                tmp[j, h, :EARLIER] = src[parent, h].astype(F32)
                dst[i, h] = jnp.where(row == EARLIER, rows_new[h][i : i + 1], tmp[j, h]).astype(BF16)

    own_f = own_query.astype(F32)
    gen = []
    for h in range(hk):
        query = own_f[h * per_head : (h + 1) * per_head].astype(BF16)
        keys = keys_out[:, h].reshape(BEAMS * BLOCK, HEAD)
        vals = values_out[:, h].reshape(BEAMS * BLOCK, HEAD)
        scores = dot_t(query, keys) * scale
        beam = lax.broadcasted_iota(jnp.int32, scores.shape, 0) % BEAMS
        owner = lax.broadcasted_iota(jnp.int32, scores.shape, 1) // BLOCK
        scores = jnp.where(beam == owner, scores, MASKED)
        top = jnp.max(scores, axis=1, keepdims=True)
        weights = jnp.exp(scores - top)
        mass = jnp.sum(weights, axis=1, keepdims=True)
        summed = jnp.dot(weights.astype(BF16), vals, preferred_element_type=F32)
        gen.append((summed, top, mass))
    gen_sum, gen_top, gen_mass = (jnp.concatenate(a, axis=0) for a in zip(*gen))

    x_q[1]()
    l_pk.wait()
    l_pv.wait()
    all_rows = n * per_head
    chunk = min(4, slots)
    queries = qall[...].astype(F32)
    inner = lax.broadcasted_iota(jnp.int32, (all_rows, BLOCK), 1)
    for h in range(hk):
        query = queries[:, h * per_head : (h + 1) * per_head].reshape(all_rows, HEAD).astype(BF16)

        def score(i, top, h=h, query=query):
            keys = pk[pl.ds(i * chunk, chunk), h].reshape(chunk * BLOCK, HEAD)
            scores = dot_t(query, keys) * scale
            low = low_b[...].reshape(all_rows, HEAD)
            high = high_b[...].reshape(all_rows, HEAD)
            for j in range(chunk):
                place = inner + table[i * chunk + j] * BLOCK
                seen = (place >= low) & (place < high)
                one = jnp.where(seen, scores[:, j * BLOCK : (j + 1) * BLOCK], MASKED)
                sbuf[i * chunk + j] = one
                top = jnp.maximum(top, one)
            return top

        top = lax.fori_loop(0, slots // chunk, score, jnp.full((all_rows, BLOCK), FLOOR, F32))
        top = jnp.max(top, axis=1, keepdims=True)

        def weigh(i, state, h=h, top=top):
            mass, summed = state
            parts = []
            for j in range(chunk):
                one = jnp.exp(sbuf[i * chunk + j] - top)
                mass = mass + one
                parts.append(one.astype(BF16))
            vals = pv[pl.ds(i * chunk, chunk), h].reshape(chunk * BLOCK, HEAD)
            summed = summed + jnp.dot(
                jnp.concatenate(parts, axis=1), vals, preferred_element_type=F32
            )
            return mass, summed

        zero = jnp.zeros((all_rows, HEAD), F32)
        mass, summed = lax.fori_loop(0, slots // chunk, weigh, (zero, zero))
        mass = jnp.sum(mass, axis=1, keepdims=True)
        some = mass > 0.0
        mean = summed / jnp.where(some, mass, 1.0)
        level = jnp.where(some, top + jnp.log(jnp.where(some, mass, 1.0)), FLOOR)
        both = jnp.concatenate([mean, split3(level, (all_rows, HEAD))], axis=1)
        sbuf2 = both.reshape(n, per_head, 2 * HEAD)
        if h == 0:
            held = [sbuf2]
        else:
            held.append(sbuf2)
    os_[...] = jnp.concatenate(held, axis=1).astype(BF16)
    orx[b] = os_[b]
    x_o[0]()
    x_o[1]()

    gen_level = gen_top + jnp.log(gen_mass)
    means = [gen_sum / gen_mass]
    levels = [gen_level]
    for t in range(n):
        got = orx[t].astype(F32)
        means.append(got[:, :HEAD])
        levels.append(got[:, HEAD : HEAD + 1] + got[:, HEAD + 1 : HEAD + 2] + got[:, HEAD + 2 : HEAD + 3])
    best = functools.reduce(jnp.maximum, levels)
    shares = [jnp.exp(level - best) for level in levels]
    whole = functools.reduce(jnp.add, shares)
    merged = functools.reduce(jnp.add, [m * s for m, s in zip(means, shares)]) / whole
    oall[b] = merged.astype(BF16)
    x_heads[0]()
    x_heads[1]()

    heads = oall[...].astype(F32)
    heads = jnp.concatenate(
        [heads[:, j * BEAMS : (j + 1) * BEAMS].reshape(rows, HEAD) for j in range(hk * GROUP)], axis=1
    ).astype(BF16)
    l_out.wait()
    kr[k] = jnp.dot(heads, wout[...], preferred_element_type=F32).astype(BF16)
    x_attn[0]()
    x_attn[1]()
    summed = kr[0].astype(F32)
    for t in range(1, z):
        summed = summed + kr[t].astype(F32)
    after = residual + summed

    squares = jnp.sum(after * after, axis=1, keepdims=True)
    normed2 = (after * mlp_norm[...]).astype(BF16)
    l_gate.wait()
    gate = jnp.dot(normed2, wgate[...], preferred_element_type=F32).reshape(n, BEAMS, units)
    l_up.wait()
    up = jnp.dot(normed2, wup[...], preferred_element_type=F32).reshape(n, BEAMS, units)
    gs[:, :, :units] = jnp.concatenate([gate, up], axis=1).astype(BF16)
    three = split3(squares, (rows, HEAD)).reshape(n, BEAMS, HEAD)
    gs[:, :, units:] = jnp.concatenate([three, three], axis=1).astype(BF16)
    gr[b] = gs[b]
    x_mix[0]()
    x_mix[1]()
    total = gr[0].astype(F32)
    for t in range(1, n):
        total = total + gr[t].astype(F32)
    three = total[:BEAMS, units:]
    squares = three[:, 0:1] + three[:, 1:2] + three[:, 2:3]
    inverse2 = lax.rsqrt(squares / MODEL_WIDTH + 1e-05)
    gate = total[:BEAMS, :units] * inverse2
    up = total[BEAMS:, :units] * inverse2
    hidden = gate / (1.0 + jnp.exp(-gate)) * up
    part_units = units // 2
    hall[b] = jnp.concatenate([hidden[:, :part_units], hidden[:, part_units:]], axis=0).astype(BF16)
    x_hid[0]()
    x_hid[1]()

    hidden = hall[...].astype(F32)
    hidden = jnp.concatenate(
        [hidden[:, :BEAMS].reshape(rows, part_units), hidden[:, BEAMS:].reshape(rows, part_units)], axis=1
    ).astype(BF16)
    l_down.wait()
    fr[k] = jnp.dot(hidden, wdown[...], preferred_element_type=F32).astype(BF16)
    x_ff[0]()
    x_ff[1]()
    summed = fr[0].astype(F32)
    for t in range(1, z):
        summed = summed + fr[t].astype(F32)
    hidden_out[0] = after + summed

    for x in (x_qkv, x_q, x_o, x_heads, x_attn, x_mix, x_hid, x_ff):
        x[2]()


def body(
    embeds, attn_norm, wqkv, w_out, mlp_norm, w_gate, w_up, w_down,
    pk, pv, gk, gv, parents, lengths, bounds, table,
):
    n = lax.axis_size("blk")
    z = lax.axis_size("kv")
    slots, hk = pk.shape[:2]
    rows, width = embeds.shape[1:]
    units = w_gate.shape[1]
    own_q = hk * GROUP * BEAMS
    smem = pl.BlockSpec(memory_space=pltpu.SMEM)
    vmem = pl.BlockSpec(memory_space=pltpu.VMEM)
    hbm = pl.BlockSpec(memory_space=pl.ANY)
    like = [pltpu.VMEM(a.shape, a.dtype) for a in (wqkv, w_out, w_gate, w_up, w_down, pk, pv, gk, gv)]
    cache = jax.ShapeDtypeStruct((BEAMS, hk, BLOCK, HEAD), BF16)
    wide = hk * COLS + HEAD
    sems = []
    for size in (n, n, n, n, z, n, n, z):
        sems += [pltpu.SemaphoreType.DMA((size,))] * 2
    return pl.pallas_call(
        functools.partial(kernel, n, z, hk, slots, width, units),
        out_shape=(jax.ShapeDtypeStruct((1, rows, width), F32), cache, cache),
        in_specs=[smem] * 4 + [vmem] * 3 + [hbm] * 9,
        out_specs=(vmem, vmem, vmem),
        scratch_shapes=like
        + [pltpu.SemaphoreType.DMA((9,))]
        + [
            pltpu.VMEM((n, BEAMS, wide), F32),
            pltpu.VMEM((n, BEAMS, wide), F32),
            pltpu.VMEM((n, own_q, HEAD), BF16),
            pltpu.VMEM((n, own_q, 2 * HEAD), BF16),
            pltpu.VMEM((n, own_q, 2 * HEAD), BF16),
            pltpu.VMEM((n, own_q, HEAD), BF16),
            pltpu.VMEM((8, 128), F32),
            pltpu.VMEM((z, rows, width), BF16),
            pltpu.VMEM((n, 2 * BEAMS, units + HEAD), BF16),
            pltpu.VMEM((n, 2 * BEAMS, units + HEAD), BF16),
            pltpu.VMEM((n, 2 * BEAMS, units // 2), BF16),
            pltpu.VMEM((8, 128), F32),
            pltpu.VMEM((z, rows, width), BF16),
            pltpu.VMEM((n, GROUP * BEAMS, HEAD), jnp.int32),
            pltpu.VMEM((n, GROUP * BEAMS, HEAD), jnp.int32),
            pltpu.VMEM((slots, n * GROUP * BEAMS, BLOCK), F32),
            pltpu.VMEM((2, hk, BLOCK, HEAD), F32),
        ]
        + sems,
        compiler_params=pltpu.CompilerParams(
            collective_id=0, has_side_effects=True, vmem_limit_bytes=56 * 2**20
        ),
        name="decode_step",
    )(
        parents, lengths, bounds, table,
        embeds, attn_norm.reshape(1, width), mlp_norm.reshape(1, width),
        wqkv, w_out, w_gate, w_up, w_down, pk, pv, gk, gv,
    )


def solution(mesh):
    in_specs = (
        P(None, None, "blk"), P("blk"), P("blk", "kv"), P("kv", "blk"), P("blk"),
        P("blk", "kv"), P("blk", "kv"), P("kv", "blk"),
        P("blk", "kv", None, None), P("blk", "kv", None, None),
        P("blk", "kv", None, None), P("blk", "kv", None, None),
        P(None, "blk"), P(), P(), P("blk"),
    )
    out_specs = (P(None, None, "blk"), P("blk", "kv", None, None), P("blk", "kv", None, None))
    return jax.shard_map(body, mesh=mesh, in_specs=in_specs, out_specs=out_specs, check_vma=False)
```

```python
import functools
import math

import jax
import jax.numpy as jnp
from jax import lax
from jax.experimental import pallas as pl
from jax.experimental.pallas import tpu as pltpu
from jax.sharding import PartitionSpec as P

MODEL_WIDTH = 3072
GROUP = 3
HEAD = 128
BEAMS = 8
TENANTS = 4
BLOCK = 128
PROMPT = 8192
EARLIER = 127
COLS = (GROUP + 2) * HEAD
MASKED = -1e30
FLOOR = -1e29
LOG2E = math.log2(math.e)
MESH = pl.DeviceIdType.MESH
F32 = jnp.float32
BF16 = jnp.bfloat16


def split3(column, shape):
    hi = column.astype(BF16).astype(F32)
    rest = column - hi
    mid = rest.astype(BF16).astype(F32)
    low = rest - mid
    lane = lax.broadcasted_iota(jnp.int32, shape, len(shape) - 1)
    return jnp.where(lane == 0, hi, jnp.where(lane == 1, mid, jnp.where(lane == 2, low, 0.0)))


def dot_t(a, b):
    return lax.dot_general(a, b, (((1,), (1,)), ((), ())), preferred_element_type=F32)


def kernel(
    n, z, hk, slots, width, units,
    parents, lengths, bounds, table,
    embeds, attn_norm, mlp_norm,
    wqkv_h, wout_h, wgate_h, wup_h, wdown_h, pk_h, pv_h, gk_h, gv_h,
    hidden_out, keys_out, values_out,
    wqkv, wout, wgate, wup, wdown, pk, pv, gk, gv, local_sem,
    qs, qr, qall, os_, orx, oall, ks, kr, ka, gs, gr, hall, fs, fr, fa,
    bias, sbuf, gkf, gvf,
    s1, r1, s2, r2, s3, r3, s4, r4, s5, r5, s6, r6, s7, r7, s8, r8, s9, r9, s10, r10,
):
    b = lax.axis_index("blk")
    k = lax.axis_index("kv")
    rows = n * BEAMS
    own_q = hk * GROUP * BEAMS
    per_head = GROUP * BEAMS
    scale = 1.0 / math.sqrt(HEAD)

    loads = [
        pltpu.make_async_copy(src, dst, local_sem.at[i])
        for i, (src, dst) in enumerate(
            [(wqkv_h, wqkv), (gk_h, gk), (gv_h, gv), (pk_h, pk), (pv_h, pv),
             (wout_h, wout), (wgate_h, wgate), (wup_h, wup), (wdown_h, wdown)]
        )
    ]
    for load in loads[:3]:
        load.start()
    l_qkv, l_gk, l_gv, l_pk, l_pv, l_out, l_gate, l_up, l_down = loads

    barrier = pltpu.get_barrier_semaphore()

    @pl.loop(1, n)
    def _(d):
        pl.semaphore_signal(barrier, inc=1, device_id={"blk": lax.rem(b + d, n)}, device_id_type=MESH)

    @pl.loop(1, z)
    def _(d):
        pl.semaphore_signal(barrier, inc=1, device_id={"kv": lax.rem(k + d, z)}, device_id_type=MESH)

    def exchange(axis, me, size, src_of, dst, ssem, rsem):
        def copy(other, slot):
            return pltpu.make_async_remote_copy(
                src_ref=src_of(other), dst_ref=dst.at[slot], send_sem=ssem.at[other],
                recv_sem=rsem.at[slot], device_id={axis: other}, device_id_type=MESH,
            )

        def each(act):
            if size <= 8:
                for d in range(1, size):
                    act(lax.rem(me + d, size))
            else:
                pl.loop(1, size)(lambda d: act(lax.rem(me + d, size)))

        def start():
            each(lambda other: copy(other, me).start())

        def arrived():
            each(lambda other: copy(other, other).wait_recv())

        def sent():
            each(lambda other: copy(other, other).wait_send())

        return start, arrived, sent

    blk = functools.partial(exchange, "blk", b, n)
    kvx = functools.partial(exchange, "kv", k, z)
    x_qkv = blk(lambda t: qs.at[t], qr, s1, r1)
    x_q = blk(lambda t: qall.at[b], qall, s2, r2)
    x_o = blk(lambda t: os_.at[t], orx, s3, r3)
    x_heads = blk(lambda t: oall.at[b], oall, s4, r4)
    x_attn = kvx(lambda t: ks.at[t], kr, s5, r5)
    x_attn2 = kvx(lambda t: ka.at[k], ka, s9, r9)
    x_mix = blk(lambda t: gs.at[t], gr, s6, r6)
    x_hid = blk(lambda t: hall.at[b], hall, s7, r7)
    x_ff = kvx(lambda t: fs.at[t], fr, s8, r8)
    x_ff2 = kvx(lambda t: fa.at[k], fa, s10, r10)

    def over_kv(part, send, got, every, scatter, gather):
        send[...] = part.reshape(send.shape).astype(BF16)
        got[k] = send[k]
        scatter[0]()
        scatter[1]()
        summed = got[0].astype(F32)
        for t in range(1, z):
            summed = summed + got[t].astype(F32)
        every[k] = summed.astype(BF16)
        gather[0]()
        gather[1]()
        return every[...].astype(F32).reshape(rows, width)

    residual = embeds[0].astype(F32)
    squares = jnp.sum(residual * residual, axis=1, keepdims=True)
    normed = (residual * attn_norm[...].reshape(1, width)).astype(BF16)
    l_qkv.wait()
    part = jnp.dot(normed, wqkv[...], preferred_element_type=F32)
    qs[:, :, : hk * COLS] = part.reshape(n, BEAMS, hk * COLS)
    qs[:, :, hk * COLS :] = jnp.broadcast_to(squares, (rows, HEAD)).reshape(n, BEAMS, HEAD)
    pl.semaphore_wait(barrier, n - 1 + z - 1)
    x_qkv[0]()

    for load in loads[3:]:
        load.start()
    lane = lax.broadcasted_iota(jnp.int32, (BEAMS, HEAD), 1)

    @pl.loop(0, n)
    def _(t):
        tenant = sum((t >= bounds[i]).astype(jnp.int32) for i in range(1, TENANTS))
        last = lengths[t]

        @pl.loop(0, slots)
        def _(i):
            place = table[i] * BLOCK - tenant * PROMPT + lane
            bias[i, t] = jnp.where((place >= 0) & (place < last), 0.0, MASKED)

    for load, src, dst in ((l_gk, gk, gkf), (l_gv, gv, gvf)):
        load.wait()
        dst[: src.shape[0]] = src[...].astype(F32)
        dst[src.shape[0] :] = jnp.zeros((8, HEAD), F32)

    half = HEAD // 2
    index = jnp.where(lane < half, lane, lane - half).astype(F32)
    freq = jnp.exp(index * (-math.log(500000.0) / half))
    position = jnp.full((BEAMS, HEAD), lengths[b] + EARLIER, jnp.int32).astype(F32)
    angle = position * freq
    cosine = jnp.cos(angle)
    sine = jnp.where(lane < half, -jnp.sin(angle), jnp.sin(angle))

    def rotated(u):
        return u * cosine + pltpu.roll(u, half, 1) * sine

    qr[b] = qs[b]
    x_qkv[1]()
    total = qr[0]
    for t in range(1, n):
        total = total + qr[t]
    inverse = lax.rsqrt(total[:, hk * COLS :] / MODEL_WIDTH + 1e-05)

    def piece(h, j):
        start = h * COLS + j * HEAD
        return total[:, start : start + HEAD] * inverse

    own_query = jnp.concatenate(
        [rotated(piece(h, g)) for h in range(hk) for g in range(GROUP)], axis=0
    ).astype(BF16)
    qall[b] = own_query
    x_q[0]()

    row = lax.broadcasted_iota(jnp.int32, (BLOCK, HEAD), 0)
    new = [
        ([rotated(piece(h, GROUP)) for h in range(hk)], gkf, keys_out),
        ([piece(h, GROUP + 1) for h in range(hk)], gvf, values_out),
    ]
    for i in range(BEAMS):
        parent = parents[0, i]
        for rows_new, src, dst in new:
            for h in range(hk):
                first = parent * (EARLIER * hk) + h
                old = src[pl.ds(first, BLOCK, stride=hk) if hk > 1 else pl.ds(first, BLOCK), :]
                dst[i, h] = jnp.where(row == EARLIER, rows_new[h][i : i + 1], old).astype(BF16)

    own_f = own_query.astype(F32)
    gen = []
    for h in range(hk):
        query = own_f[h * per_head : (h + 1) * per_head].astype(BF16)
        keys = keys_out[:, h].reshape(BEAMS * BLOCK, HEAD)
        vals = values_out[:, h].reshape(BEAMS * BLOCK, HEAD)
        scores = dot_t(query, keys) * scale
        beam = lax.broadcasted_iota(jnp.int32, scores.shape, 0) % BEAMS
        owner = lax.broadcasted_iota(jnp.int32, scores.shape, 1) // BLOCK
        scores = jnp.where(beam == owner, scores, MASKED)
        top = jnp.max(scores, axis=1, keepdims=True)
        weights = jnp.exp(scores - top)
        mass = jnp.sum(weights, axis=1, keepdims=True)
        summed = jnp.dot(weights.astype(BF16), vals, preferred_element_type=F32)
        gen.append((summed, top, mass))
    gen_sum, gen_top, gen_mass = (jnp.concatenate(a, axis=0) for a in zip(*gen))

    x_q[1]()
    l_pk.wait()
    l_pv.wait()
    all_rows = n * per_head
    chunk = min(8, slots)
    queries = qall[...].astype(F32)
    heads_q = [
        queries[:, h * per_head : (h + 1) * per_head].reshape(all_rows, HEAD).astype(BF16)
        for h in range(hk)
    ]
    zero = jnp.zeros((all_rows, HEAD), F32)
    held = []
    top = None
    for step in range(hk + 1):

        def both_passes(i, state, step=step, top=top):
            high, mass, summed = state
            if step < hk:
                keys = pk[pl.ds(i * chunk, chunk), step].reshape(chunk * BLOCK, HEAD)
                scores = dot_t(heads_q[step], keys)
                for j in range(chunk):
                    one = scores[:, j * BLOCK : (j + 1) * BLOCK].reshape(n, GROUP, BEAMS, BLOCK)
                    one = (one + bias[i * chunk + j][:, None]).reshape(all_rows, BLOCK)
                    sbuf[step % 2, i * chunk + j] = one
                    high = jnp.maximum(high, one)
            if step > 0:
                parts = []
                for j in range(chunk):
                    one = jnp.exp2((sbuf[(step - 1) % 2, i * chunk + j] - top) * (scale * LOG2E))
                    mass = mass + one
                    parts.append(one.astype(BF16))
                vals = pv[pl.ds(i * chunk, chunk), step - 1].reshape(chunk * BLOCK, HEAD)
                summed = summed + jnp.dot(
                    jnp.concatenate(parts, axis=1), vals, preferred_element_type=F32
                )
            return high, mass, summed

        floor = jnp.full((all_rows, BLOCK), FLOOR, F32)
        high, mass, summed = lax.fori_loop(0, slots // chunk, both_passes, (floor, zero, zero))
        if step > 0:
            mass = jnp.sum(mass, axis=1, keepdims=True)
            some = mass > 0.0
            safe = jnp.where(some, mass, 1.0)
            level = jnp.where(some, top * scale + jnp.log(safe), FLOOR)
            both = jnp.concatenate([summed / safe, split3(level, (all_rows, HEAD))], axis=1)
            held.append(both.reshape(n, per_head, 2 * HEAD))
        top = jnp.max(high, axis=1, keepdims=True)
    os_[...] = jnp.concatenate(held, axis=1).astype(BF16)
    orx[b] = os_[b]
    x_o[0]()
    x_o[1]()

    gen_level = gen_top + jnp.log(gen_mass)
    means = [gen_sum / gen_mass]
    levels = [gen_level]
    for t in range(n):
        got = orx[t].astype(F32)
        means.append(got[:, :HEAD])
        levels.append(got[:, HEAD : HEAD + 1] + got[:, HEAD + 1 : HEAD + 2] + got[:, HEAD + 2 : HEAD + 3])
    best = functools.reduce(jnp.maximum, levels)
    shares = [jnp.exp(level - best) for level in levels]
    whole = functools.reduce(jnp.add, shares)
    merged = functools.reduce(jnp.add, [m * s for m, s in zip(means, shares)]) / whole
    oall[b] = merged.astype(BF16)
    x_heads[0]()
    x_heads[1]()

    heads = oall[...].astype(F32)
    heads = jnp.concatenate(
        [heads[:, j * BEAMS : (j + 1) * BEAMS].reshape(rows, HEAD) for j in range(hk * GROUP)], axis=1
    ).astype(BF16)
    l_out.wait()
    after = residual + over_kv(
        jnp.dot(heads, wout[...], preferred_element_type=F32), ks, kr, ka, x_attn, x_attn2
    )

    squares = jnp.sum(after * after, axis=1, keepdims=True)
    normed2 = (after * mlp_norm[...].reshape(1, width)).astype(BF16)
    l_gate.wait()
    gate = jnp.dot(normed2, wgate[...], preferred_element_type=F32).reshape(n, BEAMS, units)
    l_up.wait()
    up = jnp.dot(normed2, wup[...], preferred_element_type=F32).reshape(n, BEAMS, units)
    gs[:, :, :units] = jnp.concatenate([gate, up], axis=1).astype(BF16)
    three = split3(squares, (rows, HEAD)).reshape(n, BEAMS, HEAD)
    gs[:, :, units:] = jnp.concatenate([three, three], axis=1).astype(BF16)
    gr[b] = gs[b]
    x_mix[0]()
    x_mix[1]()
    total = gr[0].astype(F32)
    for t in range(1, n):
        total = total + gr[t].astype(F32)
    three = total[:BEAMS, units:]
    squares = three[:, 0:1] + three[:, 1:2] + three[:, 2:3]
    inverse2 = lax.rsqrt(squares / MODEL_WIDTH + 1e-05)
    gate = total[:BEAMS, :units] * inverse2
    up = total[BEAMS:, :units] * inverse2
    hidden = gate / (1.0 + jnp.exp(-gate)) * up
    part_units = units // 2
    hall[b] = jnp.concatenate([hidden[:, :part_units], hidden[:, part_units:]], axis=0).astype(BF16)
    x_hid[0]()
    x_hid[1]()

    hidden = hall[...].astype(F32)
    hidden = jnp.concatenate(
        [hidden[:, :BEAMS].reshape(rows, part_units), hidden[:, BEAMS:].reshape(rows, part_units)], axis=1
    ).astype(BF16)
    l_down.wait()
    hidden_out[0] = after + over_kv(
        jnp.dot(hidden, wdown[...], preferred_element_type=F32), fs, fr, fa, x_ff, x_ff2
    )

    for x in (x_qkv, x_q, x_o, x_heads, x_attn, x_attn2, x_mix, x_hid, x_ff, x_ff2):
        x[2]()


def store(*refs):
    sem = refs[6]
    copies = [pltpu.make_async_copy(refs[i], refs[3 + i], sem.at[i]) for i in range(3)]
    for copy in copies:
        copy.start()
    for copy in copies:
        copy.wait()


def body(
    embeds, attn_norm, wqkv, w_out, mlp_norm, w_gate, w_up, w_down,
    pk, pv, gk, gv, parents, lengths, bounds, table,
):
    n = lax.axis_size("blk")
    z = lax.axis_size("kv")
    slots, hk = pk.shape[:2]
    rows, width = embeds.shape[1:]
    units = w_gate.shape[1]
    own_q = hk * GROUP * BEAMS
    smem = pl.BlockSpec(memory_space=pltpu.SMEM)
    vmem = pl.BlockSpec(memory_space=pltpu.VMEM)
    hbm = pl.BlockSpec(memory_space=pl.ANY)
    gk, gv = (a.transpose(0, 2, 1, 3).reshape(-1, HEAD) for a in (gk, gv))
    like = [pltpu.VMEM(a.shape, a.dtype) for a in (wqkv, w_out, w_gate, w_up, w_down, pk, pv, gk, gv)]
    cache = jax.ShapeDtypeStruct((BEAMS, hk, BLOCK, HEAD), BF16)
    wide = hk * COLS + HEAD
    sems = []
    for size in (n, n, n, n, z, n, n, z, z, z):
        sems += [pltpu.SemaphoreType.DMA((size,))] * 2
    results = pl.pallas_call(
        functools.partial(kernel, n, z, hk, slots, width, units),
        out_shape=(jax.ShapeDtypeStruct((1, rows, width), F32), cache, cache),
        in_specs=[smem] * 4 + [vmem] * 3 + [hbm] * 9,
        out_specs=(vmem, vmem, vmem),
        scratch_shapes=like
        + [pltpu.SemaphoreType.DMA((9,))]
        + [
            pltpu.VMEM((n, BEAMS, wide), F32),
            pltpu.VMEM((n, BEAMS, wide), F32),
            pltpu.VMEM((n, own_q, HEAD), BF16),
            pltpu.VMEM((n, own_q, 2 * HEAD), BF16),
            pltpu.VMEM((n, own_q, 2 * HEAD), BF16),
            pltpu.VMEM((n, own_q, HEAD), BF16),
            pltpu.VMEM((z, rows // z, width), BF16),
            pltpu.VMEM((z, rows // z, width), BF16),
            pltpu.VMEM((z, rows // z, width), BF16),
            pltpu.VMEM((n, 2 * BEAMS, units + HEAD), BF16),
            pltpu.VMEM((n, 2 * BEAMS, units + HEAD), BF16),
            pltpu.VMEM((n, 2 * BEAMS, units // 2), BF16),
            pltpu.VMEM((z, rows // z, width), BF16),
            pltpu.VMEM((z, rows // z, width), BF16),
            pltpu.VMEM((z, rows // z, width), BF16),
            pltpu.VMEM((slots, n, BEAMS, HEAD), F32),
            pltpu.VMEM((2, slots, n * GROUP * BEAMS, BLOCK), F32),
            pltpu.VMEM((gk.shape[0] + 8, HEAD), F32),
            pltpu.VMEM((gk.shape[0] + 8, HEAD), F32),
        ]
        + sems,
        compiler_params=pltpu.CompilerParams(
            collective_id=0, has_side_effects=True, vmem_limit_bytes=56 * 2**20
        ),
        name="decode_step",
    )(
        parents, lengths, bounds, table,
        embeds, attn_norm, mlp_norm,
        wqkv, w_out, w_gate, w_up, w_down, pk, pv, gk, gv,
    )
    return pl.pallas_call(
        store,
        out_shape=tuple(jax.ShapeDtypeStruct(a.shape, a.dtype) for a in results),
        in_specs=[hbm] * 3,
        out_specs=(hbm,) * 3,
        scratch_shapes=[pltpu.SemaphoreType.DMA((3,))],
        name="store_results",
    )(*results)


def solution(mesh):
    in_specs = (
        P(None, None, "blk"), P("blk"), P("blk", "kv"), P("kv", "blk"), P("blk"),
        P("blk", "kv"), P("blk", "kv"), P("kv", "blk"),
        P("blk", "kv", None, None), P("blk", "kv", None, None),
        P("blk", "kv", None, None), P("blk", "kv", None, None),
        P(None, "blk"), P(), P(), P("blk"),
    )
    out_specs = (P(None, None, "blk"), P("blk", "kv", None, None), P("blk", "kv", None, None))
    return jax.shard_map(body, mesh=mesh, in_specs=in_specs, out_specs=out_specs, check_vma=False)
```

```python
import functools
import math

import jax
import jax.numpy as jnp
from jax import lax
from jax.experimental import pallas as pl
from jax.experimental.pallas import tpu as pltpu
from jax.sharding import PartitionSpec as P

MODEL_WIDTH = 3072
GROUP = 3
HEAD = 128
BEAMS = 8
TENANTS = 4
BLOCK = 128
PROMPT = 8192
EARLIER = 127
COLS = (GROUP + 2) * HEAD
MASKED = -1e30
FLOOR = -1e29
LOG2E = math.log2(math.e)
MESH = pl.DeviceIdType.MESH
F32 = jnp.float32
BF16 = jnp.bfloat16


def split3(column, shape):
    hi = column.astype(BF16).astype(F32)
    rest = column - hi
    mid = rest.astype(BF16).astype(F32)
    low = rest - mid
    lane = lax.broadcasted_iota(jnp.int32, shape, len(shape) - 1)
    return jnp.where(lane == 0, hi, jnp.where(lane == 1, mid, jnp.where(lane == 2, low, 0.0)))


def dot_t(a, b):
    return lax.dot_general(a, b, (((1,), (1,)), ((), ())), preferred_element_type=F32)


def kernel(
    n, z, hk, slots, width, units,
    parents, lengths, bounds, table,
    embeds, attn_norm, mlp_norm,
    wqkv_h, wout_h, wgate_h, wup_h, wdown_h, pk_h, pv_h, gk_h, gv_h,
    hidden_out, keys_out, values_out,
    wqkv, wout, wgate, wup, wdown, pk, pv, gk, gv, local_sem,
    qs, qr, qall, os_, orx, oall, kr, gs, gr, hall, fr, kc, vc,
    bias, sbuf, gkf, gvf,
    s1, r1, s2, r2, s3, r3, s4, r4, s5, r5, s6, r6, s7, r7, s8, r8,
):
    b = lax.axis_index("blk")
    k = lax.axis_index("kv")
    rows = n * BEAMS
    own_q = hk * GROUP * BEAMS
    per_head = GROUP * BEAMS
    scale = 1.0 / math.sqrt(HEAD)

    barrier = pltpu.get_barrier_semaphore()

    @pl.loop(1, n)
    def _(d):
        pl.semaphore_signal(barrier, inc=1, device_id={"blk": lax.rem(b + d, n)}, device_id_type=MESH)

    @pl.loop(1, z)
    def _(d):
        pl.semaphore_signal(barrier, inc=1, device_id={"kv": lax.rem(k + d, z)}, device_id_type=MESH)

    loads = [
        pltpu.make_async_copy(src, dst, local_sem.at[i])
        for i, (src, dst) in enumerate(
            [(wqkv_h, wqkv), (gk_h, gk), (gv_h, gv), (pk_h, pk), (pv_h, pv),
             (wout_h, wout), (wgate_h, wgate), (wup_h, wup), (wdown_h, wdown)]
        )
    ]
    for load in loads[:3]:
        load.start()
    l_qkv, l_gk, l_gv, l_pk, l_pv, l_out, l_gate, l_up, l_down = loads

    def exchange(axis, me, size, src_of, dst, ssem, rsem):
        def copy(other, slot):
            return pltpu.make_async_remote_copy(
                src_ref=src_of(other), dst_ref=dst.at[slot], send_sem=ssem.at[other],
                recv_sem=rsem.at[slot], device_id={axis: other}, device_id_type=MESH,
            )

        def each(act):
            if size <= 8:
                for d in range(1, size):
                    act(lax.rem(me + d, size))
            else:
                pl.loop(1, size)(lambda d: act(lax.rem(me + d, size)))

        def start():
            each(lambda other: copy(other, me).start())

        def arrived():
            each(lambda other: copy(other, other).wait_recv())

        def sent():
            each(lambda other: copy(other, other).wait_send())

        return start, arrived, sent

    blk = functools.partial(exchange, "blk", b, n)
    kvx = functools.partial(exchange, "kv", k, z)
    x_qkv = blk(lambda t: qs.at[t], qr, s1, r1)
    x_q = blk(lambda t: qall.at[b], qall, s2, r2)
    x_o = blk(lambda t: os_.at[t], orx, s3, r3)
    x_heads = blk(lambda t: oall.at[b], oall, s4, r4)
    x_attn = kvx(lambda t: kr.at[k], kr, s5, r5)
    x_mix = blk(lambda t: gs.at[t], gr, s6, r6)
    x_hid = blk(lambda t: hall.at[b], hall, s7, r7)
    x_ff = kvx(lambda t: fr.at[k], fr, s8, r8)

    def over_kv(part, every, exchanged):
        every[k] = part.astype(BF16)
        exchanged[0]()
        exchanged[1]()
        summed = every[0].astype(F32)
        for t in range(1, z):
            summed = summed + every[t].astype(F32)
        return summed

    residual = embeds[0].astype(F32)
    squares = jnp.sum(residual * residual, axis=1, keepdims=True)
    normed = (residual * attn_norm[...].reshape(1, width)).astype(BF16)
    l_qkv.wait()
    part = jnp.dot(normed, wqkv[...], preferred_element_type=F32)
    qs[:, :, : hk * COLS] = part.reshape(n, BEAMS, hk * COLS)
    qs[:, :, hk * COLS :] = jnp.broadcast_to(squares, (rows, HEAD)).reshape(n, BEAMS, HEAD)
    pl.semaphore_wait(barrier, n - 1 + z - 1)
    x_qkv[0]()

    for load in loads[3:]:
        load.start()
    lane = lax.broadcasted_iota(jnp.int32, (BEAMS, HEAD), 1)

    firsts = [
        sum((t >= bounds[i]).astype(jnp.int32) for i in range(1, TENANTS)) * PROMPT for t in range(n)
    ]

    @pl.loop(0, slots)
    def _(i):
        start = table[i] * BLOCK
        for t in range(n):
            place = lane + (start - firsts[t])
            bias[i, t] = jnp.where((place >= 0) & (place < lengths[t]), 0.0, MASKED)

    for load, src, dst in ((l_gk, gk, gkf), (l_gv, gv, gvf)):
        load.wait()
        dst[: src.shape[0]] = src[...].astype(F32)
        dst[src.shape[0] :] = jnp.zeros((8, HEAD), F32)

    half = HEAD // 2
    index = jnp.where(lane < half, lane, lane - half).astype(F32)
    freq = jnp.exp(index * (-math.log(500000.0) / half))
    position = jnp.full((BEAMS, HEAD), lengths[b] + EARLIER, jnp.int32).astype(F32)
    angle = position * freq
    cosine = jnp.cos(angle)
    sine = jnp.where(lane < half, -jnp.sin(angle), jnp.sin(angle))

    def rotated(u):
        return u * cosine + pltpu.roll(u, half, 1) * sine

    qr[b] = qs[b]
    x_qkv[1]()
    total = qr[0]
    for t in range(1, n):
        total = total + qr[t]
    inverse = lax.rsqrt(total[:, hk * COLS :] / MODEL_WIDTH + 1e-05)

    def piece(h, j):
        start = h * COLS + j * HEAD
        return total[:, start : start + HEAD] * inverse

    own_query = jnp.concatenate(
        [rotated(piece(h, g)) for h in range(hk) for g in range(GROUP)], axis=0
    ).astype(BF16)
    qall[b] = own_query
    x_q[0]()

    row = lax.broadcasted_iota(jnp.int32, (BLOCK, HEAD), 0)
    new = [
        ([rotated(piece(h, GROUP)) for h in range(hk)], gkf, kc),
        ([piece(h, GROUP + 1) for h in range(hk)], gvf, vc),
    ]
    for i in range(BEAMS):
        parent = parents[0, i]
        for rows_new, src, dst in new:
            for h in range(hk):
                first = parent * (EARLIER * hk) + h
                old = src[pl.ds(first, BLOCK, stride=hk) if hk > 1 else pl.ds(first, BLOCK), :]
                dst[i, h] = jnp.where(row == EARLIER, rows_new[h][i : i + 1], old).astype(BF16)

    stores = [
        pltpu.make_async_copy(kc, keys_out, local_sem.at[9]),
        pltpu.make_async_copy(vc, values_out, local_sem.at[10]),
    ]
    for copy in stores:
        copy.start()
    own_f = own_query.astype(F32)
    gen = []
    for h in range(hk):
        query = own_f[h * per_head : (h + 1) * per_head].astype(BF16)
        keys = kc[:, h].reshape(BEAMS * BLOCK, HEAD)
        vals = vc[:, h].reshape(BEAMS * BLOCK, HEAD)
        scores = dot_t(query, keys) * scale
        beam = lax.broadcasted_iota(jnp.int32, scores.shape, 0) % BEAMS
        owner = lax.broadcasted_iota(jnp.int32, scores.shape, 1) // BLOCK
        scores = jnp.where(beam == owner, scores, MASKED)
        top = jnp.max(scores, axis=1, keepdims=True)
        weights = jnp.exp(scores - top)
        mass = jnp.sum(weights, axis=1, keepdims=True)
        summed = jnp.dot(weights.astype(BF16), vals, preferred_element_type=F32)
        gen.append((summed, top, mass))
    gen_sum, gen_top, gen_mass = (jnp.concatenate(a, axis=0) for a in zip(*gen))

    x_q[1]()
    l_pk.wait()
    l_pv.wait()
    all_rows = n * per_head
    chunk = min(8, slots)
    queries = qall[...].astype(F32)
    heads_q = [
        queries[:, h * per_head : (h + 1) * per_head].reshape(all_rows, HEAD).astype(BF16)
        for h in range(hk)
    ]
    zero = jnp.zeros((all_rows, HEAD), F32)
    held = []
    top = None
    for step in range(hk + 1):

        def both_passes(i, state, step=step, top=top):
            high, mass, summed = state
            if step < hk:
                keys = pk[pl.ds(i * chunk, chunk), step].reshape(chunk * BLOCK, HEAD)
                scores = dot_t(heads_q[step], keys)
                for j in range(chunk):
                    one = scores[:, j * BLOCK : (j + 1) * BLOCK].reshape(n, GROUP, BEAMS, BLOCK)
                    one = (one + bias[i * chunk + j][:, None]).reshape(all_rows, BLOCK)
                    sbuf[step % 2, i * chunk + j] = one
                    high = jnp.maximum(high, one)
            if step > 0:
                parts = []
                for j in range(chunk):
                    one = jnp.exp2((sbuf[(step - 1) % 2, i * chunk + j] - top) * (scale * LOG2E))
                    mass = mass + one
                    parts.append(one.astype(BF16))
                vals = pv[pl.ds(i * chunk, chunk), step - 1].reshape(chunk * BLOCK, HEAD)
                summed = summed + jnp.dot(
                    jnp.concatenate(parts, axis=1), vals, preferred_element_type=F32
                )
            return high, mass, summed

        floor = jnp.full((all_rows, BLOCK), FLOOR, F32)
        high, mass, summed = lax.fori_loop(0, slots // chunk, both_passes, (floor, zero, zero))
        if step > 0:
            mass = jnp.sum(mass, axis=1, keepdims=True)
            some = mass > 0.0
            safe = jnp.where(some, mass, 1.0)
            level = jnp.where(some, top * scale + jnp.log(safe), FLOOR)
            both = jnp.concatenate([summed / safe, split3(level, (all_rows, HEAD))], axis=1)
            held.append(both.reshape(n, per_head, 2 * HEAD))
        top = jnp.max(high, axis=1, keepdims=True)
    os_[...] = jnp.concatenate(held, axis=1).astype(BF16)
    orx[b] = os_[b]
    x_o[0]()
    x_o[1]()

    gen_level = gen_top + jnp.log(gen_mass)
    means = [gen_sum / gen_mass]
    levels = [gen_level]
    for t in range(n):
        got = orx[t].astype(F32)
        means.append(got[:, :HEAD])
        levels.append(got[:, HEAD : HEAD + 1] + got[:, HEAD + 1 : HEAD + 2] + got[:, HEAD + 2 : HEAD + 3])
    best = functools.reduce(jnp.maximum, levels)
    shares = [jnp.exp(level - best) for level in levels]
    whole = functools.reduce(jnp.add, shares)
    merged = functools.reduce(jnp.add, [m * s for m, s in zip(means, shares)]) / whole
    oall[b] = merged.astype(BF16)
    x_heads[0]()
    x_heads[1]()

    heads = oall[...].astype(F32)
    heads = jnp.concatenate(
        [heads[:, j * BEAMS : (j + 1) * BEAMS].reshape(rows, HEAD) for j in range(hk * GROUP)], axis=1
    ).astype(BF16)
    l_out.wait()
    after = residual + over_kv(
        jnp.dot(heads, wout[...], preferred_element_type=F32), kr, x_attn
    )

    squares = jnp.sum(after * after, axis=1, keepdims=True)
    normed2 = (after * mlp_norm[...].reshape(1, width)).astype(BF16)
    l_gate.wait()
    gate = jnp.dot(normed2, wgate[...], preferred_element_type=F32).reshape(n, BEAMS, units)
    l_up.wait()
    up = jnp.dot(normed2, wup[...], preferred_element_type=F32).reshape(n, BEAMS, units)
    gs[:, :, :units] = jnp.concatenate([gate, up], axis=1).astype(BF16)
    three = split3(squares, (rows, HEAD)).reshape(n, BEAMS, HEAD)
    gs[:, :, units:] = jnp.concatenate([three, three], axis=1).astype(BF16)
    gr[b] = gs[b]
    x_mix[0]()
    x_mix[1]()
    total = gr[0].astype(F32)
    for t in range(1, n):
        total = total + gr[t].astype(F32)
    three = total[:BEAMS, units:]
    squares = three[:, 0:1] + three[:, 1:2] + three[:, 2:3]
    inverse2 = lax.rsqrt(squares / MODEL_WIDTH + 1e-05)
    gate = total[:BEAMS, :units] * inverse2
    up = total[BEAMS:, :units] * inverse2
    hidden = gate / (1.0 + jnp.exp(-gate)) * up
    part_units = units // 2
    hall[b] = jnp.concatenate([hidden[:, :part_units], hidden[:, part_units:]], axis=0).astype(BF16)
    x_hid[0]()
    x_hid[1]()

    hidden = hall[...].astype(F32)
    hidden = jnp.concatenate(
        [hidden[:, :BEAMS].reshape(rows, part_units), hidden[:, BEAMS:].reshape(rows, part_units)], axis=1
    ).astype(BF16)
    l_down.wait()
    hidden_out[0] = after + over_kv(
        jnp.dot(hidden, wdown[...], preferred_element_type=F32), fr, x_ff
    )

    for copy in stores:
        copy.wait()
    for x in (x_qkv, x_q, x_o, x_heads, x_attn, x_mix, x_hid, x_ff):
        x[2]()


def store(*refs):
    sem = refs[6]
    copies = [pltpu.make_async_copy(refs[i], refs[3 + i], sem.at[i]) for i in range(3)]
    for copy in copies:
        copy.start()
    for copy in copies:
        copy.wait()


def body(
    embeds, attn_norm, wqkv, w_out, mlp_norm, w_gate, w_up, w_down,
    pk, pv, gk, gv, parents, lengths, bounds, table,
):
    n = lax.axis_size("blk")
    z = lax.axis_size("kv")
    slots, hk = pk.shape[:2]
    rows, width = embeds.shape[1:]
    units = w_gate.shape[1]
    own_q = hk * GROUP * BEAMS
    smem = pl.BlockSpec(memory_space=pltpu.SMEM)
    vmem = pl.BlockSpec(memory_space=pltpu.VMEM)
    hbm = pl.BlockSpec(memory_space=pl.ANY)
    gk, gv = (a.transpose(0, 2, 1, 3).reshape(-1, HEAD) for a in (gk, gv))
    like = [pltpu.VMEM(a.shape, a.dtype) for a in (wqkv, w_out, w_gate, w_up, w_down, pk, pv, gk, gv)]
    cache = jax.ShapeDtypeStruct((BEAMS, hk, BLOCK, HEAD), BF16)
    wide = hk * COLS + HEAD
    sems = []
    for size in (n, n, n, n, z, n, n, z):
        sems += [pltpu.SemaphoreType.DMA((size,))] * 2
    results = pl.pallas_call(
        functools.partial(kernel, n, z, hk, slots, width, units),
        out_shape=(jax.ShapeDtypeStruct((1, rows, width), F32), cache, cache),
        in_specs=[smem] * 4 + [vmem] * 3 + [hbm] * 9,
        out_specs=(vmem, hbm, hbm),
        scratch_shapes=like
        + [pltpu.SemaphoreType.DMA((11,))]
        + [
            pltpu.VMEM((n, BEAMS, wide), F32),
            pltpu.VMEM((n, BEAMS, wide), F32),
            pltpu.VMEM((n, own_q, HEAD), BF16),
            pltpu.VMEM((n, own_q, 2 * HEAD), BF16),
            pltpu.VMEM((n, own_q, 2 * HEAD), BF16),
            pltpu.VMEM((n, own_q, HEAD), BF16),
            pltpu.VMEM((z, rows, width), BF16),
            pltpu.VMEM((n, 2 * BEAMS, units + HEAD), BF16),
            pltpu.VMEM((n, 2 * BEAMS, units + HEAD), BF16),
            pltpu.VMEM((n, 2 * BEAMS, units // 2), BF16),
            pltpu.VMEM((z, rows, width), BF16),
            pltpu.VMEM(cache.shape, BF16),
            pltpu.VMEM(cache.shape, BF16),
            pltpu.VMEM((slots, n, BEAMS, HEAD), F32),
            pltpu.VMEM((2, slots, n * GROUP * BEAMS, BLOCK), F32),
            pltpu.VMEM((gk.shape[0] + 8, HEAD), F32),
            pltpu.VMEM((gk.shape[0] + 8, HEAD), F32),
        ]
        + sems,
        compiler_params=pltpu.CompilerParams(
            collective_id=0, has_side_effects=True, vmem_limit_bytes=56 * 2**20
        ),
        name="decode_step",
    )(
        parents, lengths, bounds, table,
        embeds, attn_norm, mlp_norm,
        wqkv, w_out, w_gate, w_up, w_down, pk, pv, gk, gv,
    )
    return pl.pallas_call(
        store,
        out_shape=tuple(jax.ShapeDtypeStruct(a.shape, a.dtype) for a in results),
        in_specs=[hbm] * 3,
        out_specs=(vmem,) * 3,
        scratch_shapes=[pltpu.SemaphoreType.DMA((3,))],
        name="store_results",
    )(*results)


def solution(mesh):
    in_specs = (
        P(None, None, "blk"), P("blk"), P("blk", "kv"), P("kv", "blk"), P("blk"),
        P("blk", "kv"), P("blk", "kv"), P("kv", "blk"),
        P("blk", "kv", None, None), P("blk", "kv", None, None),
        P("blk", "kv", None, None), P("blk", "kv", None, None),
        P(None, "blk"), P(), P(), P("blk"),
    )
    out_specs = (P(None, None, "blk"), P("blk", "kv", None, None), P("blk", "kv", None, None))
    return jax.shard_map(body, mesh=mesh, in_specs=in_specs, out_specs=out_specs, check_vma=False)
```

```python
import functools
import math

import jax
import jax.numpy as jnp
from jax import lax
from jax.experimental import pallas as pl
from jax.experimental.pallas import tpu as pltpu
from jax.sharding import PartitionSpec as P

MODEL_WIDTH = 3072
GROUP = 3
HEAD = 128
BEAMS = 8
TENANTS = 4
BLOCK = 128
PROMPT = 8192
EARLIER = 127
COLS = (GROUP + 2) * HEAD
MASKED = -1e30
FLOOR = -1e29
LOG2E = math.log2(math.e)
MESH = pl.DeviceIdType.MESH
F32 = jnp.float32
BF16 = jnp.bfloat16


def split3(column, shape):
    hi = column.astype(BF16).astype(F32)
    rest = column - hi
    mid = rest.astype(BF16).astype(F32)
    low = rest - mid
    lane = lax.broadcasted_iota(jnp.int32, shape, len(shape) - 1)
    return jnp.where(lane == 0, hi, jnp.where(lane == 1, mid, jnp.where(lane == 2, low, 0.0)))


def dot_t(a, b):
    return lax.dot_general(a, b, (((1,), (1,)), ((), ())), preferred_element_type=F32)


def kernel(
    n, z, hk, slots, width, units,
    parents, lengths, bounds, table,
    embeds, attn_norm, mlp_norm,
    wqkv_h, wout_h, wgate_h, wup_h, wdown_h, pk_h, pv_h, gk_h, gv_h,
    hidden_out, keys_out, values_out,
    wqkv, wout, wgate, wup, wdown, pk, pv, gk, gv, local_sem,
    qs, qr, qall, os_, orx, oall, kr, gs, gr, hall, fr, kc, vc,
    bias, sbuf, gkf, gvf,
    s1, r1, s2, r2, s3, r3, s4, r4, s5, r5, s6, r6, s7, r7, s8, r8,
):
    b = lax.axis_index("blk")
    k = lax.axis_index("kv")
    rows = n * BEAMS
    own_q = hk * GROUP * BEAMS
    per_head = GROUP * BEAMS
    scale = 1.0 / math.sqrt(HEAD)

    barrier = pltpu.get_barrier_semaphore()

    @pl.loop(1, n)
    def _(d):
        pl.semaphore_signal(barrier, inc=1, device_id={"blk": lax.rem(b + d, n)}, device_id_type=MESH)

    @pl.loop(1, z)
    def _(d):
        pl.semaphore_signal(barrier, inc=1, device_id={"kv": lax.rem(k + d, z)}, device_id_type=MESH)

    loads = [
        pltpu.make_async_copy(src, dst, local_sem.at[i])
        for i, (src, dst) in enumerate(
            [(wqkv_h, wqkv), (gk_h, gk), (gv_h, gv), (pk_h, pk), (pv_h, pv),
             (wout_h, wout), (wgate_h, wgate), (wup_h, wup), (wdown_h, wdown)]
        )
    ]
    for load in loads[:3]:
        load.start()
    l_qkv, l_gk, l_gv, l_pk, l_pv, l_out, l_gate, l_up, l_down = loads

    def exchange(axis, me, size, src_of, dst, ssem, rsem):
        def copy(other, slot):
            return pltpu.make_async_remote_copy(
                src_ref=src_of(other), dst_ref=dst.at[slot], send_sem=ssem.at[other],
                recv_sem=rsem.at[slot], device_id={axis: other}, device_id_type=MESH,
            )

        def each(act):
            if size <= 8:
                for d in range(1, size):
                    act(lax.rem(me + d, size))
            else:
                pl.loop(1, size)(lambda d: act(lax.rem(me + d, size)))

        def start():
            each(lambda other: copy(other, me).start())

        def arrived():
            each(lambda other: copy(other, other).wait_recv())

        def sent():
            each(lambda other: copy(other, other).wait_send())

        return start, arrived, sent

    blk = functools.partial(exchange, "blk", b, n)
    kvx = functools.partial(exchange, "kv", k, z)
    x_qkv = blk(lambda t: qs.at[t], qr, s1, r1)
    x_q = blk(lambda t: qall.at[b], qall, s2, r2)
    x_o = blk(lambda t: os_.at[t], orx, s3, r3)
    x_heads = blk(lambda t: oall.at[b], oall, s4, r4)
    x_attn = kvx(lambda t: kr.at[k], kr, s5, r5)
    x_mix = blk(lambda t: gs.at[t], gr, s6, r6)
    x_hid = blk(lambda t: hall.at[b], hall, s7, r7)
    x_ff = kvx(lambda t: fr.at[k], fr, s8, r8)

    def over_kv(part, every, exchanged):
        every[k] = part.astype(BF16)
        exchanged[0]()
        exchanged[1]()
        summed = every[0].astype(F32)
        for t in range(1, z):
            summed = summed + every[t].astype(F32)
        return summed

    residual = embeds[0].astype(F32)
    squares = jnp.sum(residual * residual, axis=1, keepdims=True)
    normed = (residual * attn_norm[...].reshape(1, width)).astype(BF16)
    l_qkv.wait()
    part = jnp.dot(normed, wqkv[...], preferred_element_type=F32)
    qs[:, :, : hk * COLS] = part.reshape(n, BEAMS, hk * COLS)
    qs[:, :, hk * COLS :] = jnp.broadcast_to(squares, (rows, HEAD)).reshape(n, BEAMS, HEAD)
    pl.semaphore_wait(barrier, n - 1 + z - 1)
    x_qkv[0]()

    for load in loads[3:]:
        load.start()
    lane = lax.broadcasted_iota(jnp.int32, (BEAMS, HEAD), 1)

    firsts = [
        sum((t >= bounds[i]).astype(jnp.int32) for i in range(1, TENANTS)) * PROMPT for t in range(n)
    ]

    @pl.loop(0, slots)
    def _(i):
        start = table[i] * BLOCK
        for t in range(n):
            place = lane + (start - firsts[t])
            bias[i, t] = jnp.where((place >= 0) & (place < lengths[t]), 0.0, MASKED)

    for load, src, dst in ((l_gk, gk, gkf), (l_gv, gv, gvf)):
        load.wait()
        dst[: src.shape[0]] = src[...].astype(F32)
        dst[src.shape[0] :] = jnp.zeros((8, HEAD), F32)

    half = HEAD // 2
    index = jnp.where(lane < half, lane, lane - half).astype(F32)
    freq = jnp.exp(index * (-math.log(500000.0) / half))
    position = jnp.full((BEAMS, HEAD), lengths[b] + EARLIER, jnp.int32).astype(F32)
    angle = position * freq
    cosine = jnp.cos(angle)
    sine = jnp.where(lane < half, -jnp.sin(angle), jnp.sin(angle))

    def rotated(u):
        return u * cosine + pltpu.roll(u, half, 1) * sine

    qr[b] = qs[b]
    x_qkv[1]()
    total = qr[0]
    for t in range(1, n):
        total = total + qr[t]
    inverse = lax.rsqrt(total[:, hk * COLS :] / MODEL_WIDTH + 1e-05)

    def piece(h, j):
        start = h * COLS + j * HEAD
        return total[:, start : start + HEAD] * inverse

    own_query = jnp.concatenate(
        [rotated(piece(h, g)) for h in range(hk) for g in range(GROUP)], axis=0
    ).astype(BF16)
    qall[b] = own_query
    x_q[0]()

    row = lax.broadcasted_iota(jnp.int32, (BLOCK, HEAD), 0)
    new = [
        ([rotated(piece(h, GROUP)) for h in range(hk)], gkf, kc),
        ([piece(h, GROUP + 1) for h in range(hk)], gvf, vc),
    ]
    for i in range(BEAMS):
        parent = parents[0, i]
        for rows_new, src, dst in new:
            for h in range(hk):
                first = parent * (EARLIER * hk) + h
                old = src[pl.ds(first, BLOCK, stride=hk) if hk > 1 else pl.ds(first, BLOCK), :]
                dst[i, h] = jnp.where(row == EARLIER, rows_new[h][i : i + 1], old).astype(BF16)

    stores = [
        pltpu.make_async_copy(kc, keys_out, local_sem.at[9]),
        pltpu.make_async_copy(vc, values_out, local_sem.at[10]),
    ]
    for copy in stores:
        copy.start()
    own_f = own_query.astype(F32)
    gen = []
    for h in range(hk):
        query = own_f[h * per_head : (h + 1) * per_head].astype(BF16)
        keys = kc[:, h].reshape(BEAMS * BLOCK, HEAD)
        vals = vc[:, h].reshape(BEAMS * BLOCK, HEAD)
        scores = dot_t(query, keys) * scale
        beam = lax.broadcasted_iota(jnp.int32, scores.shape, 0) % BEAMS
        owner = lax.broadcasted_iota(jnp.int32, scores.shape, 1) // BLOCK
        scores = jnp.where(beam == owner, scores, MASKED)
        top = jnp.max(scores, axis=1, keepdims=True)
        weights = jnp.exp(scores - top)
        mass = jnp.sum(weights, axis=1, keepdims=True)
        summed = jnp.dot(weights.astype(BF16), vals, preferred_element_type=F32)
        gen.append((summed, top, mass))
    gen_sum, gen_top, gen_mass = (jnp.concatenate(a, axis=0) for a in zip(*gen))

    x_q[1]()
    l_pk.wait()
    l_pv.wait()
    all_rows = n * per_head
    chunk = min(16, slots)
    queries = qall[...].astype(F32)
    heads_q = [
        queries[:, h * per_head : (h + 1) * per_head].reshape(all_rows, HEAD).astype(BF16)
        for h in range(hk)
    ]
    zero = jnp.zeros((all_rows, HEAD), F32)
    held = []
    top = None
    for step in range(hk + 1):

        def both_passes(i, state, step=step, top=top):
            high, mass, summed = state
            if step < hk:
                keys = pk[pl.ds(i * chunk, chunk), step].reshape(chunk * BLOCK, HEAD)
                scores = dot_t(heads_q[step], keys)
                for j in range(chunk):
                    one = scores[:, j * BLOCK : (j + 1) * BLOCK].reshape(n, GROUP, BEAMS, BLOCK)
                    one = (one + bias[i * chunk + j][:, None]).reshape(all_rows, BLOCK)
                    sbuf[step % 2, i * chunk + j] = one
                    high = jnp.maximum(high, one)
            if step > 0:
                parts = []
                for j in range(chunk):
                    one = jnp.exp2((sbuf[(step - 1) % 2, i * chunk + j] - top) * (scale * LOG2E))
                    mass = mass + one
                    parts.append(one.astype(BF16))
                vals = pv[pl.ds(i * chunk, chunk), step - 1].reshape(chunk * BLOCK, HEAD)
                summed = summed + jnp.dot(
                    jnp.concatenate(parts, axis=1), vals, preferred_element_type=F32
                )
            return high, mass, summed

        floor = jnp.full((all_rows, BLOCK), FLOOR, F32)
        high, mass, summed = lax.fori_loop(0, slots // chunk, both_passes, (floor, zero, zero))
        if step > 0:
            mass = jnp.sum(mass, axis=1, keepdims=True)
            some = mass > 0.0
            safe = jnp.where(some, mass, 1.0)
            level = jnp.where(some, top * scale + jnp.log(safe), FLOOR)
            both = jnp.concatenate([summed / safe, split3(level, (all_rows, HEAD))], axis=1)
            held.append(both.reshape(n, per_head, 2 * HEAD))
        top = jnp.max(high, axis=1, keepdims=True)
    os_[...] = jnp.concatenate(held, axis=1).astype(BF16)
    orx[b] = os_[b]
    x_o[0]()
    x_o[1]()

    gen_level = gen_top + jnp.log(gen_mass)
    means = [gen_sum / gen_mass]
    levels = [gen_level]
    for t in range(n):
        got = orx[t].astype(F32)
        means.append(got[:, :HEAD])
        levels.append(got[:, HEAD : HEAD + 1] + got[:, HEAD + 1 : HEAD + 2] + got[:, HEAD + 2 : HEAD + 3])
    best = functools.reduce(jnp.maximum, levels)
    shares = [jnp.exp(level - best) for level in levels]
    whole = functools.reduce(jnp.add, shares)
    merged = functools.reduce(jnp.add, [m * s for m, s in zip(means, shares)]) / whole
    oall[b] = merged.astype(BF16)
    x_heads[0]()
    x_heads[1]()

    heads = oall[...].astype(F32)
    heads = jnp.concatenate(
        [heads[:, j * BEAMS : (j + 1) * BEAMS].reshape(rows, HEAD) for j in range(hk * GROUP)], axis=1
    ).astype(BF16)
    l_out.wait()
    after = residual + over_kv(
        jnp.dot(heads, wout[...], preferred_element_type=F32), kr, x_attn
    )

    squares = jnp.sum(after * after, axis=1, keepdims=True)
    normed2 = (after * mlp_norm[...].reshape(1, width)).astype(BF16)
    l_gate.wait()
    gate = jnp.dot(normed2, wgate[...], preferred_element_type=F32).reshape(n, BEAMS, units)
    l_up.wait()
    up = jnp.dot(normed2, wup[...], preferred_element_type=F32).reshape(n, BEAMS, units)
    gs[:, :, :units] = jnp.concatenate([gate, up], axis=1).astype(BF16)
    three = split3(squares, (rows, HEAD)).reshape(n, BEAMS, HEAD)
    gs[:, :, units:] = jnp.concatenate([three, three], axis=1).astype(BF16)
    gr[b] = gs[b]
    x_mix[0]()
    x_mix[1]()
    total = gr[0].astype(F32)
    for t in range(1, n):
        total = total + gr[t].astype(F32)
    three = total[:BEAMS, units:]
    squares = three[:, 0:1] + three[:, 1:2] + three[:, 2:3]
    inverse2 = lax.rsqrt(squares / MODEL_WIDTH + 1e-05)
    gate = total[:BEAMS, :units] * inverse2
    up = total[BEAMS:, :units] * inverse2
    hidden = gate / (1.0 + jnp.exp(-gate)) * up
    part_units = units // 2
    hall[b] = jnp.concatenate([hidden[:, :part_units], hidden[:, part_units:]], axis=0).astype(BF16)
    x_hid[0]()
    x_hid[1]()

    hidden = hall[...].astype(F32)
    hidden = jnp.concatenate(
        [hidden[:, :BEAMS].reshape(rows, part_units), hidden[:, BEAMS:].reshape(rows, part_units)], axis=1
    ).astype(BF16)
    l_down.wait()
    hidden_out[0] = after + over_kv(
        jnp.dot(hidden, wdown[...], preferred_element_type=F32), fr, x_ff
    )

    for copy in stores:
        copy.wait()
    for x in (x_qkv, x_q, x_o, x_heads, x_attn, x_mix, x_hid, x_ff):
        x[2]()


def store(*refs):
    sem = refs[6]
    copies = [pltpu.make_async_copy(refs[i], refs[3 + i], sem.at[i]) for i in range(3)]
    for copy in copies:
        copy.start()
    for copy in copies:
        copy.wait()


def body(
    embeds, attn_norm, wqkv, w_out, mlp_norm, w_gate, w_up, w_down,
    pk, pv, gk, gv, parents, lengths, bounds, table,
):
    n = lax.axis_size("blk")
    z = lax.axis_size("kv")
    slots, hk = pk.shape[:2]
    rows, width = embeds.shape[1:]
    units = w_gate.shape[1]
    own_q = hk * GROUP * BEAMS
    smem = pl.BlockSpec(memory_space=pltpu.SMEM)
    vmem = pl.BlockSpec(memory_space=pltpu.VMEM)
    hbm = pl.BlockSpec(memory_space=pl.ANY)
    gk, gv = (a.transpose(0, 2, 1, 3).reshape(-1, HEAD) for a in (gk, gv))
    like = [pltpu.VMEM(a.shape, a.dtype) for a in (wqkv, w_out, w_gate, w_up, w_down, pk, pv, gk, gv)]
    cache = jax.ShapeDtypeStruct((BEAMS, hk, BLOCK, HEAD), BF16)
    wide = hk * COLS + HEAD
    sems = []
    for size in (n, n, n, n, z, n, n, z):
        sems += [pltpu.SemaphoreType.DMA((size,))] * 2
    results = pl.pallas_call(
        functools.partial(kernel, n, z, hk, slots, width, units),
        out_shape=(jax.ShapeDtypeStruct((1, rows, width), F32), cache, cache),
        in_specs=[smem] * 4 + [vmem] * 3 + [hbm] * 9,
        out_specs=(vmem, hbm, hbm),
        scratch_shapes=like
        + [pltpu.SemaphoreType.DMA((11,))]
        + [
            pltpu.VMEM((n, BEAMS, wide), F32),
            pltpu.VMEM((n, BEAMS, wide), F32),
            pltpu.VMEM((n, own_q, HEAD), BF16),
            pltpu.VMEM((n, own_q, 2 * HEAD), BF16),
            pltpu.VMEM((n, own_q, 2 * HEAD), BF16),
            pltpu.VMEM((n, own_q, HEAD), BF16),
            pltpu.VMEM((z, rows, width), BF16),
            pltpu.VMEM((n, 2 * BEAMS, units + HEAD), BF16),
            pltpu.VMEM((n, 2 * BEAMS, units + HEAD), BF16),
            pltpu.VMEM((n, 2 * BEAMS, units // 2), BF16),
            pltpu.VMEM((z, rows, width), BF16),
            pltpu.VMEM(cache.shape, BF16),
            pltpu.VMEM(cache.shape, BF16),
            pltpu.VMEM((slots, n, BEAMS, HEAD), F32),
            pltpu.VMEM((2, slots, n * GROUP * BEAMS, BLOCK), F32),
            pltpu.VMEM((gk.shape[0] + 8, HEAD), F32),
            pltpu.VMEM((gk.shape[0] + 8, HEAD), F32),
        ]
        + sems,
        compiler_params=pltpu.CompilerParams(
            collective_id=0, has_side_effects=True, vmem_limit_bytes=56 * 2**20
        ),
        name="decode_step",
    )(
        parents, lengths, bounds, table,
        embeds, attn_norm, mlp_norm,
        wqkv, w_out, w_gate, w_up, w_down, pk, pv, gk, gv,
    )
    return pl.pallas_call(
        store,
        out_shape=tuple(jax.ShapeDtypeStruct(a.shape, a.dtype) for a in results),
        in_specs=[hbm] * 3,
        out_specs=(vmem,) * 3,
        scratch_shapes=[pltpu.SemaphoreType.DMA((3,))],
        name="store_results",
    )(*results)


def solution(mesh):
    in_specs = (
        P(None, None, "blk"), P("blk"), P("blk", "kv"), P("kv", "blk"), P("blk"),
        P("blk", "kv"), P("blk", "kv"), P("kv", "blk"),
        P("blk", "kv", None, None), P("blk", "kv", None, None),
        P("blk", "kv", None, None), P("blk", "kv", None, None),
        P(None, "blk"), P(), P(), P("blk"),
    )
    out_specs = (P(None, None, "blk"), P("blk", "kv", None, None), P("blk", "kv", None, None))
    return jax.shard_map(body, mesh=mesh, in_specs=in_specs, out_specs=out_specs, check_vma=False)
```
